32 devices in a mesh: ctx: 16 (over z, x, core), head: 2 (over y).
Axes of the slice: x: 2, y: 2, z: 4, core: 2. Of those that a mesh axis runs over, the one named last changes fastest.
Arguments:
- queries: bfloat16 [4096, 1024], P('ctx', 'head'), may hold values from -6 to 6
- key_rows: bfloat16 [4096, 256], P('ctx', 'head'), may hold values from -6 to 6
- value_rows: bfloat16 [4096, 256], P('ctx', 'head'), may hold values from -6 to 6
- attn_out: bfloat16 [4096, 1024], P('ctx', 'head'), may hold values from -6 to 6
- out_grad: bfloat16 [4096, 1024], P('ctx', 'head'), may hold values from -6 to 6
- log_sums: float32 [8, 4096], P('head', 'ctx'), may hold values from 4.5 to 6
- block_picks: int32 [32, 8, 3], P('ctx', 'head'), may hold values from 0 to 3, all different within a row
- query_weight: bfloat16 [4096, 1024], P('ctx', 'head'), may hold values from -0.21875 to 0.21875
- key_weight: bfloat16 [4096, 256], P('ctx', 'head'), may hold values from -0.21875 to 0.21875
- value_weight: bfloat16 [4096, 256], P('ctx', 'head'), may hold values from -0.21875 to 0.21875
Outputs:
- input_grad: bfloat16 [4096, 4096], P('ctx', 'head')
The draws below stay inside these ranges and needn't reach their ends.
Inputs may be any that keep to these rules, and one draw needn't show every extreme that they name: `block_picks`: in each row (query block, query head) the 3 entries differ; entry m selects the block m + 1 blocks before the query's block, and selections before the sequence's start select nothing.
All inputs are finite; a program needn't handle non-finite values.
Results may differ from the reference program's by a relative error of at most 0.013.
Values may be sent and summed in bfloat16 or wider, within the bound.
A program may use at most 64 MiB of HBM per device.

```python
import math
import jax
import jax.numpy as jnp
from jax import lax

D = 4096
HD = 128
GROUP = 4
BLK = 128
TOPK = 3
KV_HEADS = 2
QHEADS = 8
TOKENS = 4096
NQB = 32
WINDOW = 4


def steps_of(own_key, dims, split, least, high):
    def one(axis_at, shards_of):
        heights = jax.random.uniform(jax.random.fold_in(jax.random.fold_in(own_key, 6), axis_at), (shards_of,), jnp.float32, least / len(split), high / len(split))
        return jnp.repeat(jnp.exp(heights), dims[axis_at] // shards_of).reshape((-1,) + (1,) * (len(dims) - axis_at - 1))

    level = one(*split[0])
    for cut in split[1:]:
        level = level * one(*cut)
    return level


def picks_of(own_key, rows, amount, top, lift):
    order = jax.random.permutation(jax.random.fold_in(own_key, 1), amount)
    pull = order
    for power in range(3):
        pull = pull * pull // amount
    pull = pull * lift // amount
    lots = jax.random.randint(jax.random.fold_in(own_key, 2), (rows, amount), 0, 4096) + pull
    holders = jax.random.permutation(jax.random.fold_in(own_key, 3), rows)[jnp.arange(amount) % rows]
    lots = jnp.where(jnp.arange(rows)[:, None] == holders[None, :], 1 << 14, lots)
    score = lots * amount + jnp.arange(amount)
    return lax.top_k(score.astype(jnp.int32), top)[1].astype(jnp.int32)


def noise(rng, shape, spread, most, shards=(), kind=jnp.bfloat16):
    drawn = spread * jax.random.normal(rng, shape, jnp.float32)
    if shards:
        drawn = drawn * steps_of(rng, shape, shards, -0.22, 0.18)
    return jnp.clip(drawn, -most, most).astype(kind)


def setup_inputs(seed: int = 0) -> dict:
    key_of = jax.random.split(jax.random.key(seed), 11)
    queries = noise(key_of[0], (TOKENS, QHEADS * HD), 1.0, 6.0, ((0, 16), (1, 2)))
    key_rows = noise(key_of[1], (TOKENS, KV_HEADS * HD), 1.0, 6.0, ((0, 16), (1, 2)))
    value_rows = noise(key_of[2], (TOKENS, KV_HEADS * HD), 1.0, 6.0, ((0, 16), (1, 2)))
    attn_out = noise(key_of[3], (TOKENS, QHEADS * HD), 1.0, 6.0, ((0, 16), (1, 2)))
    out_grad = noise(key_of[4], (TOKENS, QHEADS * HD), 1.0, 6.0, ((0, 16), (1, 2)))
    log_sums = jnp.clip(4.5 + 1.5 * jax.random.uniform(key_of[5], (QHEADS, TOKENS), jnp.float32) ** steps_of(key_of[5], (QHEADS, TOKENS), ((0, 2), (1, 16)), -0.2, 0.2), 4.5, 6.0)
    block_picks = picks_of(key_of[6], NQB * QHEADS, WINDOW, TOPK, 6144).reshape((NQB, QHEADS, TOPK))
    query_weight = noise(key_of[7], (D, QHEADS * HD), ((GROUP + 2) * HD) ** -0.5, 0.21875, ((0, 16), (1, 2)))
    key_weight = noise(key_of[8], (D, KV_HEADS * HD), ((GROUP + 2) * HD) ** -0.5, 0.21875, ((0, 16), (1, 2)))
    value_weight = noise(key_of[9], (D, KV_HEADS * HD), ((GROUP + 2) * HD) ** -0.5, 0.21875, ((0, 16), (1, 2)))
    return dict(queries=queries, key_rows=key_rows, value_rows=value_rows, attn_out=attn_out, out_grad=out_grad, log_sums=log_sums, block_picks=block_picks, query_weight=query_weight, key_weight=key_weight, value_weight=value_weight)


def rounded(values_in):
    return lax.optimization_barrier(values_in.astype(jnp.bfloat16)).astype(jnp.float32)

def head_grads(query_part, grad_part, log_part, delta_part, pick_part, key_table, value_table):
    blocks, width, group, head_dim = query_part.shape
    scaling = 1.0 / math.sqrt(head_dim)
    offsets = jnp.concatenate([jnp.zeros((blocks, group, 1), jnp.int32), pick_part.astype(jnp.int32) + 1], axis=2)
    key_block = jnp.arange(blocks, dtype=jnp.int32)[:, None, None] - offsets
    usable = key_block >= 0
    clipped = jnp.clip(key_block, 0, blocks - 1).astype(jnp.int32)
    key_sel = key_table[clipped]
    value_sel = value_table[clipped]
    scores = jnp.einsum('bqgd,bgskd->bgqsk', query_part, key_sel) * scaling
    position = jnp.arange(width)
    causal = position[:, None] >= position[None, :]
    allowed = usable[:, :, None, :, None] & ((offsets != 0)[:, :, None, :, None] | causal[None, None, :, None, :])
    probability = jnp.where(allowed, jnp.exp(scores - log_part[:, :, :, None, None]), 0.0)
    prob_grad = jnp.einsum('bqgd,bgskd->bgqsk', grad_part, value_sel)
    score_grad = probability * (prob_grad - delta_part[:, :, :, None, None])
    prob_half = rounded(probability)
    grad_half = rounded(score_grad)
    query_grad = jnp.einsum('bgqsk,bgskd->bqgd', grad_half, key_sel) * scaling
    key_terms = jnp.einsum('bgqsk,bqgd->bgskd', grad_half, query_part) * scaling
    value_terms = jnp.einsum('bgqsk,bqgd->bgskd', prob_half, grad_part)
    flat_index = clipped.reshape(-1)
    key_grad = jax.ops.segment_sum(key_terms.reshape(-1, width, head_dim), flat_index, num_segments=blocks)
    value_grad = jax.ops.segment_sum(value_terms.reshape(-1, width, head_dim), flat_index, num_segments=blocks)
    return (query_grad, key_grad, value_grad)

def reference(queries, key_rows, value_rows, attn_out, out_grad, log_sums, block_picks, query_weight, key_weight, value_weight):
    blocks = TOKENS // BLK
    stacked = (queries.reshape(blocks, BLK, KV_HEADS, GROUP, HD).transpose(2, 0, 1, 3, 4), out_grad.reshape(blocks, BLK, KV_HEADS, GROUP, HD).transpose(2, 0, 1, 3, 4), attn_out.reshape(blocks, BLK, KV_HEADS, GROUP, HD).transpose(2, 0, 1, 3, 4), key_rows.reshape(blocks, BLK, KV_HEADS, HD).transpose(2, 0, 1, 3), value_rows.reshape(blocks, BLK, KV_HEADS, HD).transpose(2, 0, 1, 3), log_sums.reshape(KV_HEADS, GROUP, blocks, BLK).transpose(0, 2, 1, 3), block_picks.reshape(blocks, KV_HEADS, GROUP, TOPK).transpose(1, 0, 2, 3), query_weight.reshape(D, KV_HEADS, GROUP * HD).transpose(1, 0, 2), key_weight.reshape(D, KV_HEADS, HD).transpose(1, 0, 2), value_weight.reshape(D, KV_HEADS, HD).transpose(1, 0, 2))

    def step_head(total, items):
        query_part, grad_part, out_part, key_part, value_part, log_part, pick_part, query_proj, key_proj, value_proj = items
        query_full = query_part.astype(jnp.float32)
        grad_full = grad_part.astype(jnp.float32)
        delta_part = lax.optimization_barrier(jnp.sum(grad_full * out_part.astype(jnp.float32), axis=3)).transpose(0, 2, 1)
        query_grad, key_grad, value_grad = head_grads(query_full, grad_full, log_part, delta_part, pick_part, key_part.astype(jnp.float32), value_part.astype(jnp.float32))
        grads = jnp.concatenate([query_grad.reshape(TOKENS, GROUP * HD).astype(jnp.bfloat16), key_grad.reshape(TOKENS, HD).astype(jnp.bfloat16), value_grad.reshape(TOKENS, HD).astype(jnp.bfloat16)], axis=1)
        weight_cat = jnp.concatenate([query_proj, key_proj, value_proj], axis=1)
        partial_value = jnp.dot(grads, weight_cat.T, preferred_element_type=jnp.float32)
        return (total + rounded(partial_value), None)
    total, unused = lax.scan(step_head, jnp.zeros((TOKENS, D), jnp.float32), stacked)
    return total.astype(jnp.bfloat16)
```

```python
import functools
import math

import jax
import jax.numpy as jnp
from jax import lax
from jax.experimental import pallas as pl
from jax.experimental.pallas import tpu as pltpu
from jax.sharding import PartitionSpec as P

BLK = 128
WINDOW = 4
MESH = pl.DeviceIdType.MESH
NEG = -1e30


def dot_nt(a, b):
    return lax.dot_general(a, b, (((1,), (1,)), ((), ())), preferred_element_type=jnp.float32)


def dot_nn(a, b):
    return lax.dot_general(a, b, (((1,), (0,)), ((), ())), preferred_element_type=jnp.float32)


def kernel(
    ctx, heads, group, hd, far,
    q_hbm, k_hbm, v_hbm, o_hbm, g_hbm, lse_ref, picks_ref, wq_hbm, wk_hbm, wv_hbm,
    out_ref,
    w, q, g, o, kv, pt, dst, acc, ksend, krecv, grads, part, got,
    local_sem, halo_send, halo_recv, back_send, back_recv,
    ring_send, ring_recv, sib_send, sib_recv, part_send, part_recv,
):
    i = lax.axis_index("ctx")
    me = lax.axis_index("head")
    tokens = q.shape[0]
    blocks = tokens // BLK
    rows = w.shape[1]
    half = rows // 2
    cols = group * hd
    scaling = 1.0 / math.sqrt(hd)
    chips = ctx // 2
    depth = chips // 2
    steps = chips // 2
    core = i % 2
    chip = i // 2
    side = chip % 2
    at = (chip // 2) * (1 - side) + (chips - 1 - chip // 2) * side

    def owner(pos):
        pos = (pos + chips) % chips
        high = pos // depth
        return 2 * ((1 - high) * 2 * pos + high * (2 * (chips - 1 - pos) + 1)) + core

    up, down = owner(at + 1), owner(at - 1)
    sibling = i + 1 - 2 * core

    local = [
        pltpu.make_async_copy(wq_hbm, w.at[i, :, pl.ds(0, cols)], local_sem.at[0]),
        pltpu.make_async_copy(wk_hbm, w.at[i, :, pl.ds(cols, hd)], local_sem.at[1]),
        pltpu.make_async_copy(wv_hbm, w.at[i, :, pl.ds(cols + hd, hd)], local_sem.at[2]),
        pltpu.make_async_copy(k_hbm, kv.at[far, 0], local_sem.at[3]),
        pltpu.make_async_copy(v_hbm, kv.at[far, 1], local_sem.at[4]),
        pltpu.make_async_copy(q_hbm, q, local_sem.at[5]),
        pltpu.make_async_copy(g_hbm, g, local_sem.at[6]),
        pltpu.make_async_copy(o_hbm, o, local_sem.at[7]),
    ]
    for copy in (local[3], local[4], *local[:3], *local[5:]):
        copy.start()

    barrier = pltpu.get_barrier_semaphore()
    peers = [(up, me), (down, me), (sibling, me)]
    for d in range(1, far + 1):
        peers += [((i + d) % ctx, me), ((i + ctx - d) % ctx, me)]
    for d in range(1, heads):
        peers.append((i, (me + d) % heads))
    for peer in peers:
        pl.semaphore_signal(barrier, inc=1, device_id=peer, device_id_type=MESH)
    for d in range(1, far + 1):

        @pl.when(i < d)
        def _():
            kv[far - d] = jnp.zeros_like(kv[far - d])

        @pl.when(i + d >= ctx)
        def _():
            krecv[d - 1] = jnp.zeros_like(krecv[d - 1])

    pl.semaphore_wait(barrier, len(peers))

    def remote(src, dest, ssem, rsem, to):
        return pltpu.make_async_remote_copy(
            src_ref=src, dst_ref=dest, send_sem=ssem, recv_sem=rsem,
            device_id=to, device_id_type=MESH,
        )

    def halo(d):
        return remote(kv.at[far], kv.at[far - d], halo_send.at[d - 1], halo_recv.at[d - 1],
                      ((i + d) % ctx, me))

    def back(d):
        return remote(ksend.at[d - 1], krecv.at[d - 1], back_send.at[d - 1], back_recv.at[d - 1],
                      ((i + ctx - d) % ctx, me))

    def ring(way, step, piece, shard):
        ref = w.at[shard, pl.ds(piece * half, half)]
        return remote(ref, ref, ring_send.at[way, step - 1, piece], ring_recv.at[way, step - 1, piece],
                      (up if way == 0 else down, me))

    def share(slot, shard):
        return remote(w.at[shard], w.at[shard], sib_send.at[slot], sib_recv.at[slot], (sibling, me))

    def pieces(way, step):
        return (0, 1) if step < steps else (way,)

    def source(way, step):
        return owner(at - step) if way == 0 else owner(at + step)

    def other(shard):
        return shard + 1 - 2 * core

    local[3].wait()
    local[4].wait()
    for d in range(1, far + 1):

        @pl.when(i + d < ctx)
        def _():
            halo(d).start()

    for copy in local[:3]:
        copy.wait()
    for piece in (0, 1):
        for way in (0, 1):
            if piece in pieces(way, 1):
                ring(way, 1, piece, i).start()
    share(0, i).start()
    for copy in local[5:]:
        copy.wait()

    acc[...] = jnp.zeros_like(acc)
    for d in range(1, far + 1):

        @pl.when(i >= d)
        def _():
            halo(d).wait_recv()

    first = far * blocks - WINDOW
    row_id = lax.broadcasted_iota(jnp.int32, (BLK, BLK), 0)
    col_id = lax.broadcasted_iota(jnp.int32, (BLK, BLK), 1)
    causal_one = row_id <= col_id
    causal = jnp.concatenate([causal_one] * group, axis=1)

    def table(which, block):
        return kv[block // blocks, which, pl.ds((block % blocks) * BLK, BLK), :]

    for b in range(blocks):
        span = pl.ds(b * BLK, BLK)
        qs = jnp.concatenate([q[span, pl.ds(h * hd, hd)] for h in range(group)], axis=0)
        gs = jnp.concatenate([g[span, pl.ds(h * hd, hd)] for h in range(group)], axis=0)
        delta = jnp.concatenate(
            [
                jnp.sum(
                    (
                        g[span, pl.ds(h * hd, hd)].astype(jnp.float32)
                        * o[span, pl.ds(h * hd, hd)].astype(jnp.float32)
                    ).T,
                    axis=0,
                    keepdims=True,
                )
                for h in range(group)
            ],
            axis=1,
        )
        for m in range(WINDOW + 1):
            away = WINDOW - m
            shifts = []
            for h in range(group):
                piece = -lse_ref[pl.ds(h, 1), span]
                if away:
                    hit = picks_ref[b, h, 0] == away - 1
                    for c in range(1, picks_ref.shape[2]):
                        hit = jnp.logical_or(hit, picks_ref[b, h, c] == away - 1)
                    hit = jnp.logical_and(hit, i * blocks + b >= away)
                    piece = piece + jnp.where(hit, 0.0, NEG)
                shifts.append(piece)
            shift = jnp.concatenate(shifts, axis=1)
            key = table(0, first + b + m)
            value = table(1, first + b + m)
            p = jnp.exp(dot_nt(key, qs) * scaling + shift)
            if not away:
                p = jnp.where(causal, p, 0.0)
            ds = p * (dot_nt(value, gs) - delta)
            pt[pl.ds(m * BLK, BLK), :] = p.astype(jnp.bfloat16)
            dst[pl.ds(m * BLK, BLK), :] = ds.astype(jnp.bfloat16)
        window = pl.ds((first + b) * BLK, (WINDOW + 1) * BLK)
        dsv = dst[...]
        acc[0, window, :] += dot_nn(dsv, qs)
        acc[1, window, :] += dot_nn(pt[...], gs)
        keys_t = jnp.concatenate(
            [table(0, first + b + m) for m in range(WINDOW + 1)], axis=0
        ).T
        dq = dot_nn(keys_t, dsv) * scaling
        for h in range(group):
            grads[span, pl.ds(h * hd, hd)] = dq[:, h * BLK : (h + 1) * BLK].T.astype(jnp.bfloat16)

    for d in range(1, far + 1):
        span = pl.ds((far - d) * tokens, tokens)
        ksend[d - 1, 0] = (acc[0, span, :] * scaling).astype(jnp.bfloat16)
        ksend[d - 1, 1] = acc[1, span, :].astype(jnp.bfloat16)

        @pl.when(i >= d)
        def _():
            back(d).start()

    def advance(step):
        for piece in (0, 1):
            for way in (0, 1):
                if piece in pieces(way, step):
                    shard = source(way, step)
                    ring(way, step, piece, shard).wait_recv()
                    if step < steps and piece in pieces(way, step + 1):
                        ring(way, step + 1, piece, shard).start()
        for way in (0, 1) if step < steps else (0,):
            share(2 * step - 1 + way, source(way, step)).start()

    advance(1)

    for d in range(1, far + 1):

        @pl.when(i + d < ctx)
        def _():
            back(d).wait_recv()

    own = pl.ds(far * tokens, tokens)
    dk = acc[0, own, :] * scaling
    dv = acc[1, own, :]
    for d in range(1, far + 1):
        dk += krecv[d - 1, 0].astype(jnp.float32)
        dv += krecv[d - 1, 1].astype(jnp.float32)
    grads[:, pl.ds(cols, hd)] = dk.astype(jnp.bfloat16)
    grads[:, pl.ds(cols + hd, hd)] = dv.astype(jnp.bfloat16)

    per = ctx // heads

    def handing(shard):
        return remote(part.at[shard], got.at[me, shard % per], part_send.at[shard],
                      part_recv.at[me, shard % per], (i, shard // per))

    def project(shard):
        part[shard] = dot_nt(grads[...], w[shard]).astype(jnp.bfloat16)

        @pl.when(shard // per != me)
        def _():
            handing(shard).start()

    project(i)
    share(0, other(i)).wait_recv()
    project(other(i))
    for step in range(1, steps + 1):
        ways = (0, 1) if step < steps else (0,)
        if step > 1:
            advance(step)
        for way in ways:
            project(source(way, step))
        for way in ways:
            shard = other(source(way, step))
            share(2 * step - 1 + way, shard).wait_recv()
            project(shard)

    for l in range(per):
        total = part[me * per + l].astype(jnp.float32)
        for d in range(1, heads):
            giver = (me + d) % heads
            remote(got.at[giver, l], got.at[giver, l], part_send.at[0], part_recv.at[giver, l],
                   (i, giver)).wait_recv()
            total += got[giver, l].astype(jnp.float32)
        out_ref[:, pl.ds(l * rows, rows)] = total.astype(jnp.bfloat16)

    for d in range(1, far + 1):

        @pl.when(i + d < ctx)
        def _():
            halo(d).wait_send()

        @pl.when(i >= d)
        def _():
            back(d).wait_send()

    for step in range(1, steps + 1):
        for way in (0, 1):
            for piece in pieces(way, step):
                ring(way, step, piece, source(way, step - 1)).wait_send()
    for slot in range(2 * steps):
        share(slot, i).wait_send()
    for shard in range(ctx):

        @pl.when(shard // per != me)
        def _():
            handing(shard).wait_send()


def per_device(ctx, heads, queries, key_rows, value_rows, attn_out, out_grad, log_sums,
               block_picks, query_weight, key_weight, value_weight):
    tokens, cols = queries.shape
    hd = key_rows.shape[1]
    group = cols // hd
    blocks = tokens // BLK
    far = -(-WINDOW // blocks)
    rows = query_weight.shape[0]
    width = cols + 2 * hd
    steps = ctx // 4
    per = ctx // heads
    bf, f32 = jnp.bfloat16, jnp.float32
    dma = pltpu.SemaphoreType.DMA
    hbm = pl.BlockSpec(memory_space=pl.ANY)
    return pl.pallas_call(
        functools.partial(kernel, ctx, heads, group, hd, far),
        out_shape=jax.ShapeDtypeStruct((tokens, per * rows), bf),
        in_specs=[hbm] * 5
        + [pl.BlockSpec(memory_space=pltpu.VMEM), pl.BlockSpec(memory_space=pltpu.SMEM)]
        + [hbm] * 3,
        out_specs=pl.BlockSpec(memory_space=pltpu.VMEM),
        scratch_shapes=[
            pltpu.VMEM((ctx, rows, width), bf),
            pltpu.VMEM((tokens, cols), bf),
            pltpu.VMEM((tokens, cols), bf),
            pltpu.VMEM((tokens, cols), bf),
            pltpu.VMEM((far + 1, 2, tokens, hd), bf),
            pltpu.VMEM(((WINDOW + 1) * BLK, group * BLK), bf),
            pltpu.VMEM(((WINDOW + 1) * BLK, group * BLK), bf),
            pltpu.VMEM((2, (far + 1) * tokens, hd), f32),
            pltpu.VMEM((far, 2, tokens, hd), bf),
            pltpu.VMEM((far, 2, tokens, hd), bf),
            pltpu.VMEM((tokens, width), bf),
            pltpu.VMEM((ctx, tokens, rows), bf),
            pltpu.VMEM((heads, per, tokens, rows), bf),
            dma((8,)), dma((far,)), dma((far,)), dma((far,)), dma((far,)),
            dma((2, steps, 2)), dma((2, steps, 2)),
            dma((2 * steps,)), dma((2 * steps,)),
            dma((ctx,)), dma((heads, per)),
        ],
        compiler_params=pltpu.CompilerParams(
            collective_id=0, has_side_effects=True, vmem_limit_bytes=56 * 1024 * 1024
        ),
    )(queries, key_rows, value_rows, attn_out, out_grad, log_sums, block_picks,
      query_weight, key_weight, value_weight)


def solution(mesh):
    placed = (
        P("ctx", "head"),
        P("ctx", "head"),
        P("ctx", "head"),
        P("ctx", "head"),
        P("ctx", "head"),
        P("head", "ctx"),
        P("ctx", "head", None),
        P("ctx", "head"),
        P("ctx", "head"),
        P("ctx", "head"),
    )
    body = functools.partial(per_device, mesh.shape["ctx"], mesh.shape["head"])
    return jax.shard_map(
        body, mesh=mesh, in_specs=placed, out_specs=P("ctx", "head"), check_vma=False
    )
```

```python
import functools
import math

import jax
import jax.numpy as jnp
from jax import lax
from jax.experimental import pallas as pl
from jax.experimental.pallas import tpu as pltpu
from jax.sharding import PartitionSpec as P

BLK = 128
WINDOW = 4
MESH = pl.DeviceIdType.MESH
NEG = -1e30


def dot_nt(a, b):
    return lax.dot_general(a, b, (((1,), (1,)), ((), ())), preferred_element_type=jnp.float32)


def dot_nn(a, b):
    return lax.dot_general(a, b, (((1,), (0,)), ((), ())), preferred_element_type=jnp.float32)


def kernel(
    ctx, heads, group, hd, far,
    q_hbm, k_hbm, v_hbm, o_hbm, g_hbm, lse_ref, picks_ref, wq_hbm, wk_hbm, wv_hbm,
    out_ref,
    w, q, g, o, kv, pt, dst, acc, ksend, krecv, grads, part, got,
    local_sem, halo_send, halo_recv, back_send, back_recv,
    ring_send, ring_recv, sib_send, sib_recv, part_send, part_recv,
):
    i = lax.axis_index("ctx")
    me = lax.axis_index("head")
    tokens = q.shape[0]
    blocks = tokens // BLK
    rows = w.shape[1]
    half = rows // 2
    cols = group * hd
    scaling = 1.0 / math.sqrt(hd)
    chips = ctx // 2
    depth = chips // 2
    steps = chips // 2
    core = i % 2
    chip = i // 2
    side = chip % 2
    at = (chip // 2) * (1 - side) + (chips - 1 - chip // 2) * side

    def owner(pos):
        pos = (pos + chips) % chips
        high = pos // depth
        return 2 * ((1 - high) * 2 * pos + high * (2 * (chips - 1 - pos) + 1)) + core

    up, down = owner(at + 1), owner(at - 1)
    sibling = i + 1 - 2 * core

    local = [
        pltpu.make_async_copy(wq_hbm, w.at[i, :, pl.ds(0, cols)], local_sem.at[0]),
        pltpu.make_async_copy(wk_hbm, w.at[i, :, pl.ds(cols, hd)], local_sem.at[1]),
        pltpu.make_async_copy(wv_hbm, w.at[i, :, pl.ds(cols + hd, hd)], local_sem.at[2]),
        pltpu.make_async_copy(k_hbm, kv.at[far, 0], local_sem.at[3]),
        pltpu.make_async_copy(v_hbm, kv.at[far, 1], local_sem.at[4]),
        pltpu.make_async_copy(q_hbm, q, local_sem.at[5]),
        pltpu.make_async_copy(g_hbm, g, local_sem.at[6]),
        pltpu.make_async_copy(o_hbm, o, local_sem.at[7]),
    ]
    for copy in (local[3], local[4], *local[:3], *local[5:]):
        copy.start()

    barrier = pltpu.get_barrier_semaphore()
    peers = [(up, me), (down, me), (sibling, me)]
    for d in range(1, far + 1):
        peers += [((i + d) % ctx, me), ((i + ctx - d) % ctx, me)]
    for d in range(1, heads):
        peers.append((i, (me + d) % heads))
    for peer in peers:
        pl.semaphore_signal(barrier, inc=1, device_id=peer, device_id_type=MESH)
    for d in range(1, far + 1):

        @pl.when(i < d)
        def _():
            kv[far - d] = jnp.zeros_like(kv[far - d])

        @pl.when(i + d >= ctx)
        def _():
            krecv[d - 1] = jnp.zeros_like(krecv[d - 1])

    pl.semaphore_wait(barrier, len(peers))

    def remote(src, dest, ssem, rsem, to):
        return pltpu.make_async_remote_copy(
            src_ref=src, dst_ref=dest, send_sem=ssem, recv_sem=rsem,
            device_id=to, device_id_type=MESH,
        )

    def halo(d):
        return remote(kv.at[far], kv.at[far - d], halo_send.at[d - 1], halo_recv.at[d - 1],
                      ((i + d) % ctx, me))

    def back(d):
        return remote(ksend.at[d - 1], krecv.at[d - 1], back_send.at[d - 1], back_recv.at[d - 1],
                      ((i + ctx - d) % ctx, me))

    def ring(way, step, piece, shard):
        ref = w.at[shard, pl.ds(piece * half, half)]
        return remote(ref, ref, ring_send.at[way, step - 1, piece], ring_recv.at[way, step - 1, piece],
                      (up if way == 0 else down, me))

    def share(slot, shard):
        return remote(w.at[shard], w.at[shard], sib_send.at[slot], sib_recv.at[slot], (sibling, me))

    def pieces(way, step):
        return (0, 1) if step < steps else (way,)

    def source(way, step):
        return owner(at - step) if way == 0 else owner(at + step)

    def other(shard):
        return shard + 1 - 2 * core

    local[3].wait()
    local[4].wait()
    for d in range(1, far + 1):

        @pl.when(i + d < ctx)
        def _():
            halo(d).start()

    for copy in local[:3]:
        copy.wait()
    for way in (0, 1):
        ring(way, 1, pieces(way, 1)[0], i).start()
    share(0, i).start()
    for copy in local[5:]:
        copy.wait()

    acc[...] = jnp.zeros_like(acc)
    for d in range(1, far + 1):

        @pl.when(i >= d)
        def _():
            halo(d).wait_recv()

    first = far * blocks - WINDOW
    row_id = lax.broadcasted_iota(jnp.int32, (BLK, BLK), 0)
    col_id = lax.broadcasted_iota(jnp.int32, (BLK, BLK), 1)
    causal_one = row_id <= col_id
    causal = jnp.concatenate([causal_one] * group, axis=1)

    def table(which, block):
        return kv[block // blocks, which, pl.ds((block % blocks) * BLK, BLK), :]

    for b in range(blocks):
        span = pl.ds(b * BLK, BLK)
        qs = jnp.concatenate([q[span, pl.ds(h * hd, hd)] for h in range(group)], axis=0)
        gs = jnp.concatenate([g[span, pl.ds(h * hd, hd)] for h in range(group)], axis=0)
        delta = jnp.concatenate(
            [
                jnp.sum(
                    (
                        g[span, pl.ds(h * hd, hd)].astype(jnp.float32)
                        * o[span, pl.ds(h * hd, hd)].astype(jnp.float32)
                    ).T,
                    axis=0,
                    keepdims=True,
                )
                for h in range(group)
            ],
            axis=1,
        )
        for m in range(WINDOW + 1):
            away = WINDOW - m
            shifts = []
            for h in range(group):
                piece = -lse_ref[pl.ds(h, 1), span]
                if away:
                    hit = picks_ref[b, h, 0] == away - 1
                    for c in range(1, picks_ref.shape[2]):
                        hit = jnp.logical_or(hit, picks_ref[b, h, c] == away - 1)
                    hit = jnp.logical_and(hit, i * blocks + b >= away)
                    piece = piece + jnp.where(hit, 0.0, NEG)
                shifts.append(piece)
            shift = jnp.concatenate(shifts, axis=1)
            key = table(0, first + b + m)
            value = table(1, first + b + m)
            p = jnp.exp(dot_nt(key, qs) * scaling + shift)
            if not away:
                p = jnp.where(causal, p, 0.0)
            ds = p * (dot_nt(value, gs) - delta)
            pt[pl.ds(m * BLK, BLK), :] = p.astype(jnp.bfloat16)
            dst[pl.ds(m * BLK, BLK), :] = ds.astype(jnp.bfloat16)
        window = pl.ds((first + b) * BLK, (WINDOW + 1) * BLK)
        dsv = dst[...]
        acc[0, window, :] += dot_nn(dsv, qs)
        acc[1, window, :] += dot_nn(pt[...], gs)
        keys_t = jnp.concatenate(
            [table(0, first + b + m) for m in range(WINDOW + 1)], axis=0
        ).T
        dq = dot_nn(keys_t, dsv) * scaling
        for h in range(group):
            grads[span, pl.ds(h * hd, hd)] = dq[:, h * BLK : (h + 1) * BLK].T.astype(jnp.bfloat16)

    for d in range(1, far + 1):
        span = pl.ds((far - d) * tokens, tokens)
        ksend[d - 1, 0] = (acc[0, span, :] * scaling).astype(jnp.bfloat16)
        ksend[d - 1, 1] = acc[1, span, :].astype(jnp.bfloat16)

        @pl.when(i >= d)
        def _():
            back(d).start()

    def advance(step):
        for piece in (0, 1):
            for way in (0, 1):
                if piece in pieces(way, step):
                    shard = source(way, step)
                    ring(way, step, piece, shard).wait_recv()
                    if step < steps and piece in pieces(way, step + 1):
                        ring(way, step + 1, piece, shard).start()
        for way in (0, 1) if step < steps else (0,):
            share(2 * step - 1 + way, source(way, step)).start()

    for way in (0, 1):
        for piece in pieces(way, 1)[1:]:
            ring(way, 1, piece, i).start()

    advance(1)

    for d in range(1, far + 1):

        @pl.when(i + d < ctx)
        def _():
            back(d).wait_recv()

    own = pl.ds(far * tokens, tokens)
    dk = acc[0, own, :] * scaling
    dv = acc[1, own, :]
    for d in range(1, far + 1):
        dk += krecv[d - 1, 0].astype(jnp.float32)
        dv += krecv[d - 1, 1].astype(jnp.float32)
    grads[:, pl.ds(cols, hd)] = dk.astype(jnp.bfloat16)
    grads[:, pl.ds(cols + hd, hd)] = dv.astype(jnp.bfloat16)

    per = ctx // heads

    def handing(shard):
        return remote(part.at[shard], got.at[me, shard % per], part_send.at[shard],
                      part_recv.at[me, shard % per], (i, shard // per))

    def project(shard):
        part[shard] = dot_nt(grads[...], w[shard]).astype(jnp.bfloat16)

        @pl.when(shard // per != me)
        def _():
            handing(shard).start()

    project(i)
    share(0, other(i)).wait_recv()
    project(other(i))
    for step in range(1, steps + 1):
        ways = (0, 1) if step < steps else (0,)
        if step > 1:
            advance(step)
        for way in ways:
            project(source(way, step))
        for way in ways:
            shard = other(source(way, step))
            share(2 * step - 1 + way, shard).wait_recv()
            project(shard)

    for l in range(per):
        total = part[me * per + l].astype(jnp.float32)
        for d in range(1, heads):
            giver = (me + d) % heads
            remote(got.at[giver, l], got.at[giver, l], part_send.at[0], part_recv.at[giver, l],
                   (i, giver)).wait_recv()
            total += got[giver, l].astype(jnp.float32)
        out_ref[:, pl.ds(l * rows, rows)] = total.astype(jnp.bfloat16)

    for d in range(1, far + 1):

        @pl.when(i + d < ctx)
        def _():
            halo(d).wait_send()

        @pl.when(i >= d)
        def _():
            back(d).wait_send()

    for step in range(1, steps + 1):
        for way in (0, 1):
            for piece in pieces(way, step):
                ring(way, step, piece, source(way, step - 1)).wait_send()
    for slot in range(2 * steps):
        share(slot, i).wait_send()
    for shard in range(ctx):

        @pl.when(shard // per != me)
        def _():
            handing(shard).wait_send()


def per_device(ctx, heads, queries, key_rows, value_rows, attn_out, out_grad, log_sums,
               block_picks, query_weight, key_weight, value_weight):
    tokens, cols = queries.shape
    hd = key_rows.shape[1]
    group = cols // hd
    blocks = tokens // BLK
    far = -(-WINDOW // blocks)
    rows = query_weight.shape[0]
    width = cols + 2 * hd
    steps = ctx // 4
    per = ctx // heads
    bf, f32 = jnp.bfloat16, jnp.float32
    dma = pltpu.SemaphoreType.DMA
    hbm = pl.BlockSpec(memory_space=pl.ANY)
    return pl.pallas_call(
        functools.partial(kernel, ctx, heads, group, hd, far),
        out_shape=jax.ShapeDtypeStruct((tokens, per * rows), bf),
        in_specs=[hbm] * 5
        + [pl.BlockSpec(memory_space=pltpu.VMEM), pl.BlockSpec(memory_space=pltpu.SMEM)]
        + [hbm] * 3,
        out_specs=pl.BlockSpec(memory_space=pltpu.VMEM),
        scratch_shapes=[
            pltpu.VMEM((ctx, rows, width), bf),
            pltpu.VMEM((tokens, cols), bf),
            pltpu.VMEM((tokens, cols), bf),
            pltpu.VMEM((tokens, cols), bf),
            pltpu.VMEM((far + 1, 2, tokens, hd), bf),
            pltpu.VMEM(((WINDOW + 1) * BLK, group * BLK), bf),
            pltpu.VMEM(((WINDOW + 1) * BLK, group * BLK), bf),
            pltpu.VMEM((2, (far + 1) * tokens, hd), f32),
            pltpu.VMEM((far, 2, tokens, hd), bf),
            pltpu.VMEM((far, 2, tokens, hd), bf),
            pltpu.VMEM((tokens, width), bf),
            pltpu.VMEM((ctx, tokens, rows), bf),
            pltpu.VMEM((heads, per, tokens, rows), bf),
            dma((8,)), dma((far,)), dma((far,)), dma((far,)), dma((far,)),
            dma((2, steps, 2)), dma((2, steps, 2)),
            dma((2 * steps,)), dma((2 * steps,)),
            dma((ctx,)), dma((heads, per)),
        ],
        compiler_params=pltpu.CompilerParams(
            collective_id=0, has_side_effects=True, vmem_limit_bytes=56 * 1024 * 1024
        ),
    )(queries, key_rows, value_rows, attn_out, out_grad, log_sums, block_picks,
      query_weight, key_weight, value_weight)


def solution(mesh):
    placed = (
        P("ctx", "head"),
        P("ctx", "head"),
        P("ctx", "head"),
        P("ctx", "head"),
        P("ctx", "head"),
        P("head", "ctx"),
        P("ctx", "head", None),
        P("ctx", "head"),
        P("ctx", "head"),
        P("ctx", "head"),
    )
    body = functools.partial(per_device, mesh.shape["ctx"], mesh.shape["head"])
    return jax.shard_map(
        body, mesh=mesh, in_specs=placed, out_specs=P("ctx", "head"), check_vma=False
    )
```
